32 devices in a mesh: inlet: 4 (over y, x), row: 8 (over z, core).
Axes of the slice: x: 2, y: 2, z: 4, core: 2. Of those that a mesh axis runs over, the one named last changes fastest.
Arguments:
- coeffs: float32 [4, 1024, 1024], P('inlet', 'row'), may hold values from -6 to 6
- basis: float32 [4, 2048, 3, 1024], P('inlet', 'row'), may hold values from -0.1875 to 0.1875
- route: int32 [8192, 1], P(('inlet', 'row')), may hold values from 0 to 31; in each aligned block of 256 rows (0 to 255, 256 to 511, ...) at most 12 rows name the same one
Outputs:
- inflow: bfloat16 [12288, 3, 1024], P(('inlet', 'row'))
The draws below stay inside these ranges and needn't reach their ends.
Inputs may be any that keep to these rules, and one draw needn't show every extreme that they name: `route`: among the rows of one device, no owner is named more than 12 times, a bound that some block reaches.
All inputs are finite; a program needn't handle non-finite values.
Results may differ from the reference program's by a relative error of at most 0.001.
Values may be sent and summed in bfloat16 or wider, within the bound.
A program may use at most 64 MiB of HBM per device.

```python
import math
import jax
import jax.numpy as jnp
import numpy as np
from jax import lax

MODES = 1024
STEPS = 1024
PTS_DEV = 256
INLETS = 4
PTS_INLET = 2048
CAP = 12
N_INLET = 4
N_ROW = 8


def shard_levels(stream_key, dims, shards, smallest, high):
    def one(position, parts):
        draws = jax.random.uniform(jax.random.fold_in(jax.random.fold_in(stream_key, 6), position), (parts,), jnp.float32, smallest / len(shards), high / len(shards))
        return jnp.repeat(jnp.exp(draws), dims[position] // parts).reshape((-1,) + (1,) * (len(dims) - position - 1))

    factor_of = one(*shards[0])
    for cut in shards[1:]:
        factor_of = factor_of * one(*cut)
    return factor_of


def routed_block(own_key, own, number, rows, number_of, top, reach, lean):
    order = jax.random.permutation(own_key, number_of)
    heavy_load, common = load_shares(number_of, rows * top, reach, lean, True), load_shares(number_of, rows * top, reach, lean, False)
    places = jnp.arange(number_of)

    def named(lengths, rotation):
        used = int((lengths > 0).sum())
        fixed = max(1, used // 4)
        shifted = fixed + (places - fixed + rotation * (used - fixed)) % max(1, number_of - fixed)
        return jnp.zeros((number_of,), jnp.int32).at[order[jnp.where(places < fixed, places, shifted)]].set(jnp.asarray(lengths, jnp.int32))

    lengths = jnp.where(number % 4 == 0, named(heavy_load, number // 4), named(common, number - number // 4 - 1))
    mixed = jax.random.permutation(jax.random.fold_in(own, 3), number_of)
    giver, sink = mixed[0:number_of // 2 * 2:2], mixed[1:number_of // 2 * 2:2]
    room = jnp.minimum(lengths[giver] - 1, reach - lengths[sink]) // 2
    room = jnp.where((giver == order[0]) | (sink == order[0]) | (lengths[sink] == 0), 0, jnp.maximum(room, 0))
    shifted = jax.random.randint(jax.random.fold_in(own, 4), (number_of // 2,), 0, 1 << 20) % (room + 1)
    lengths = lengths.at[giver].add(-shifted).at[sink].add(shifted)
    members = jnp.searchsorted(jnp.cumsum(lengths), jnp.arange(rows * top), side="right").astype(jnp.int32)
    table = members.reshape(top, rows).T
    table = table[jax.random.permutation(jax.random.fold_in(own, 1), rows)]
    rotation = jax.random.randint(jax.random.fold_in(own, 2), (rows, 1), 0, top)
    return jnp.take_along_axis(table, (jnp.arange(top)[None, :] + rotation) % top, axis=1)


def load_shares(amount, total, most, skew, full):
    weights = [(1 << 20) // math.isqrt(standing ** skew) + 1 for standing in range(1, amount + 1)]
    largest = most if full else min(most, max(-(-total // amount), total * weights[0] // sum(weights)))
    least = 1 if total - largest >= amount - 1 else 0
    counts, rest = [largest] + [least] * (amount - 1), total - largest - least * (amount - 1)
    while rest > 0:
        candidates = [i for i in range(1, amount) if counts[i] < largest] or [i for i in range(1, amount) if counts[i] < most]
        pool, budget = sum([weights[i] for i in candidates]), rest
        for i in candidates:
            addition = min(most - counts[i], max(1, budget * weights[i] // pool), rest)
            counts[i] = counts[i] + addition
            rest = rest - addition
    return np.array(counts)


def bell_draw(stream_key, shape, width, reach, split=(), kind=jnp.bfloat16):
    factor_of = shard_levels(stream_key, shape, split, -0.22, 0.18) if split else 1.0
    values = jax.random.normal(stream_key, shape, jnp.float32) * width * factor_of
    return jnp.minimum(jnp.maximum(values, -reach), reach).astype(kind)


def setup_inputs(seed: int = 0) -> dict:
    seeds = jax.random.split(jax.random.key(seed), 4)
    coeffs = bell_draw(seeds[0], (INLETS, STEPS, MODES), 1.0, 6.0, ((0, 4), (1, 8)), jnp.float32)
    basis = bell_draw(seeds[1], (INLETS, PTS_INLET, 3, MODES), MODES ** -0.5, 0.1875, ((0, 4), (1, 8)), jnp.float32)
    route_keys = jax.random.split(jax.random.fold_in(seeds[2], 1), (INLETS * PTS_INLET) // PTS_DEV)
    route_turns = jax.random.permutation(jax.random.fold_in(seeds[2], 3), (INLETS * PTS_INLET) // PTS_DEV)
    route = jax.vmap(lambda own, number: routed_block(jax.random.fold_in(seeds[2], 2), own, number, PTS_DEV, N_INLET * N_ROW, 1, CAP, 2))(route_keys, route_turns).reshape((INLETS * PTS_INLET, 1))
    return {"coeffs": coeffs, "basis": basis, "route": route}


def reference(coeffs, basis, route):
    count = N_INLET * N_ROW
    per_source = basis.reshape(count, PTS_DEV, 3, MODES)
    owners = route.reshape(count, PTS_DEV)
    result = jnp.zeros((count, count, CAP, 3 * STEPS), jnp.bfloat16)

    def place(source, result):
        source = jnp.asarray(source).astype(jnp.int32)
        inlet_index = (source // N_ROW).astype(jnp.int32)
        block = lax.dynamic_index_in_dim(per_source, source, 0, keepdims=False)
        panel = lax.dynamic_index_in_dim(coeffs, inlet_index, 0, keepdims=False)
        velocity = jnp.einsum("pcm,tm->pct", block, panel, precision=lax.Precision.HIGHEST)
        velocity = velocity.astype(jnp.bfloat16).reshape(PTS_DEV, 3 * STEPS)
        owner = lax.dynamic_index_in_dim(owners, source, 0, keepdims=False)
        onehot = (owner[:, None] == jnp.arange(count, dtype=jnp.int32)[None, :]).astype(jnp.int32)
        running = jnp.cumsum(onehot, axis=0)
        rank = jnp.sum(onehot * running, axis=1) - 1
        slot = (owner * CAP + rank).astype(jnp.int32)
        packed = jnp.zeros((count * CAP, 3 * STEPS), jnp.bfloat16).at[slot].set(velocity)
        packed = packed.reshape(count, 1, CAP, 3 * STEPS)
        zero = jnp.int32(0)
        return lax.dynamic_update_slice(result, packed, (zero, source, zero, zero))

    result = lax.fori_loop(0, count, place, result)
    return result.reshape(count * count * CAP, 3, STEPS)
```

```python
import jax
import jax.numpy as jnp
from jax import lax
from jax.sharding import PartitionSpec as P


def slots(route, capacity):
    owner = route[:, 0]
    place = jnp.arange(owner.shape[0], dtype=jnp.int32)
    before = (owner[:, None] == owner[None, :]) & (place[:, None] < place[None, :])
    return owner * capacity + jnp.sum(before.astype(jnp.int32), axis=0)


def local(coeffs, basis, route):
    points = basis.shape[1]
    count = lax.axis_size(("inlet", "row"))
    capacity = 3 * points // (2 * count)
    panel = lax.all_gather(coeffs, "row", axis=1, tiled=True)[0]
    steps = panel.shape[0]
    slot = slots(route, capacity).reshape(1, points)
    onehot = (jnp.arange(count * capacity, dtype=jnp.int32)[:, None] == slot).astype(jnp.float32)
    packed = jnp.einsum("sp,pcm->csm", onehot, basis[0], precision=lax.Precision.HIGHEST)
    packed = packed.reshape(3, count, capacity, -1).transpose(1, 0, 2, 3).reshape(count * 3 * capacity, -1)
    velocity = jnp.einsum("sm,tm->st", packed, panel, precision=lax.Precision.HIGH)
    velocity = velocity.astype(jnp.bfloat16).reshape(count, 3 * capacity, steps)
    moved = lax.all_to_all(velocity, ("inlet", "row"), split_axis=0, concat_axis=0, tiled=True)
    moved = moved.reshape(count, 3, capacity, steps).transpose(0, 2, 1, 3)
    return moved.reshape(count * capacity, 3, steps)


def solution(mesh):
    in_specs = (P("inlet", "row", None), P("inlet", "row", None, None), P(("inlet", "row"), None))
    out_specs = P(("inlet", "row"), None, None)
    return jax.shard_map(local, mesh=mesh, in_specs=in_specs, out_specs=out_specs, check_vma=False)
```

```python
import jax
import jax.numpy as jnp
import numpy as np
from jax import lax
from jax.experimental import pallas as pl
from jax.experimental.pallas import tpu as pltpu
from jax.sharding import PartitionSpec as P

MESH = pl.DeviceIdType.MESH
CAPACITY, ROWS, REST, WIDE = 12, 32, 4, 256
F32, BF16 = jnp.float32, jnp.bfloat16
NT = (((1,), (1,)), ((), ()))


def halves(x):
    high = x.astype(BF16)
    return high, (x - high.astype(F32)).astype(BF16)


def exchange(coeffs, basis, slot, main, rest, panel, base_h, base_l, pack_h, pack_l, pan_h, pan_l, out, rest32, out_rest,
             g_send, g_recv, own_sem, a_send, a_recv, x_send, x_recv):
    inlet, row = lax.axis_index("inlet"), lax.axis_index("row")
    me = inlet * 8 + row
    z, core = row // 2, row % 2

    def step(kind, zc, src):
        target = (row + 2, row - 2, z * 2 + 1 - core)[kind]
        return pltpu.make_async_remote_copy(
            src_ref=src, dst_ref=panel.at[zc * 2 + core], send_sem=g_send.at[kind, zc],
            recv_sem=g_recv.at[zc * 2 + core], device_id=(inlet, target), device_id_type=MESH)

    def arrived(chunk):
        pltpu.make_async_copy(panel.at[chunk], panel.at[chunk], g_recv.at[chunk]).wait()

    def sends(zc):
        return ((zc <= z) & (z < 3), (zc >= z) & (z > 0))

    @pl.when(z < 3)
    def _():
        step(0, z, coeffs).start()

    @pl.when(z > 0)
    def _():
        step(1, z, coeffs).start()

    step(2, z, coeffs).start()
    own = pltpu.make_async_copy(coeffs, panel.at[row], own_sem)
    own.start()

    @pl.loop(0, 3)
    def _(c):
        at = pl.ds(pl.multiple_of(c * 256, 256), 256)
        high, low = halves(basis[at, :])
        base_h[at, :] = high
        base_l[at, :] = low

    points = jnp.broadcast_to(slot[...], (128, 256))

    @pl.loop(0, 9)
    def _(tile):
        line = lax.broadcasted_iota(jnp.int32, (128, 256), 0) + tile * 128
        q = line & 31
        c = (q >= 12).astype(jnp.int32) + (q >= 24).astype(jnp.int32)
        key = (line >> 5) * CAPACITY + q - 12 * c
        tail = line - 32 * ROWS
        in_tail = tail >= 0
        key = jnp.where(in_tail, (tail & 31) * CAPACITY + 8 + (tail >> 5), key)
        c = jnp.where(in_tail, 2, c)
        hit = key == points
        pick = jnp.concatenate(
            [jnp.where(hit & (c == k), 1.0, 0.0).astype(BF16) for k in range(3)], axis=1)
        at = pl.ds(pl.multiple_of(tile * 128, 128), 128)
        pack_h[at, :] = jnp.dot(pick, base_h[...], preferred_element_type=F32).astype(BF16)
        pack_l[at, :] = jnp.dot(pick, base_l[...], preferred_element_type=F32).astype(BF16)

    def product(at):
        total = lax.dot_general(pack_h[at, :], pan_h[...], NT, preferred_element_type=F32)
        total += lax.dot_general(pack_l[at, :], pan_h[...], NT, preferred_element_type=F32)
        return total + lax.dot_general(pack_h[at, :], pan_l[...], NT, preferred_element_type=F32)

    def piece(zc, owner):
        return pltpu.make_async_remote_copy(
            src_ref=out.at[zc, owner], dst_ref=main.at[zc, me], send_sem=a_send.at[zc], recv_sem=a_recv.at[zc],
            device_id=(owner // 8, owner % 8), device_id_type=MESH)

    def last(owner):
        return pltpu.make_async_remote_copy(
            src_ref=out_rest.at[owner], dst_ref=rest.at[me], send_sem=x_send, recv_sem=x_recv,
            device_id=(owner // 8, owner % 8), device_id_type=MESH)

    for k in range(4):
        near = [(0, 1, 2, 3), (1, 0, 2, 3), (2, 3, 1, 0), (3, 2, 1, 0)]
        zc = jnp.where(z == 0, near[0][k], jnp.where(z == 1, near[1][k], jnp.where(z == 2, near[2][k], near[3][k])))
        if k == 0:
            own.wait()
        else:
            arrived(zc * 2 + core)
            right, left = sends(zc)

            @pl.when(right)
            def _():
                step(0, zc, panel.at[zc * 2 + core]).start()

            @pl.when(left)
            def _():
                step(1, zc, panel.at[zc * 2 + core]).start()

            step(2, zc, panel.at[zc * 2 + core]).start()
        arrived(zc * 2 + 1 - core)
        for part in range(2):
            high, low = halves(panel[zc * 2 + part])
            pan_h[part * 128:part * 128 + 128, :] = high
            pan_l[part * 128:part * 128 + 128, :] = low

        @pl.loop(0, 4)
        def _(turn):
            group = (turn + inlet) % 4
            at = pl.ds(pl.multiple_of(group * 256, 256), 256)
            out[zc, pl.ds(group * 8, 8)] = product(at).astype(BF16).reshape(8, ROWS, WIDE)

            @pl.loop(0, 8)
            def _(j):
                owner = group * 8 + (j + row) % 8

                @pl.when(owner != me)
                def _():
                    piece(zc, owner).start()

                @pl.when(owner == me)
                def _():
                    pltpu.make_async_copy(out.at[zc, me], main.at[zc, me], a_recv.at[zc]).start()

        tail = product(pl.ds(32 * ROWS, 32 * REST))
        for e in range(REST):
            for part in range(2):
                rest32[pl.ds(e * 8 + zc * 2 + part, 32, stride=32), :] = (
                    tail[e * 32:e * 32 + 32, part * 128:part * 128 + 128])

    out_rest[...] = rest32[...].astype(BF16).reshape(32, 32, 128)

    @pl.loop(0, 32)
    def _(j):
        owner = (j + me) % 32

        @pl.when(owner != me)
        def _():
            last(owner).start()

        @pl.when(owner == me)
        def _():
            pltpu.make_async_copy(out_rest.at[me], rest.at[me], x_recv).start()

    for zc in range(4):
        right, left = sends(zc)

        @pl.when(right)
        def _():
            step(0, zc, coeffs).wait_send()

        @pl.when(left)
        def _():
            step(1, zc, coeffs).wait_send()

        step(2, zc, coeffs).wait_send()
        some = out.at[zc, pl.ds(0, 31)]
        pltpu.make_async_copy(some, some, a_send.at[zc]).wait()
        pltpu.make_async_copy(main.at[zc], main.at[zc], a_recv.at[zc]).wait()
    some = out_rest.at[pl.ds(0, 31)]
    pltpu.make_async_copy(some, some, x_send).wait()
    pltpu.make_async_copy(rest, rest, x_recv).wait()


def settle(pick_main, pick_rest, main, rest, inflow):
    for zc in range(4):
        at = slice(zc * WIDE, zc * WIDE + WIDE)
        block = jnp.dot(pick_main[...], main[zc].reshape(4 * ROWS, WIDE), preferred_element_type=F32)
        block += jnp.dot(pick_rest[...], rest[:, at], preferred_element_type=F32)
        inflow[:, :, at] = block.astype(BF16).reshape(3, 48, WIDE)


def picks():
    full = np.zeros((144, 4 * 36), np.float32)
    for c in range(3):
        for s in range(4):
            for r in range(CAPACITY):
                q = c * CAPACITY + r
                full[c * 48 + s * CAPACITY + r, s * ROWS + q if q < ROWS else 4 * ROWS + s * REST + q - ROWS] = 1
    return jnp.asarray(full[:, :4 * ROWS], BF16), jnp.asarray(full[:, 4 * ROWS:], BF16)


def fused(coeffs, basis, route):
    slot = slots(route, CAPACITY).reshape(1, 256)
    rows = basis[0].transpose(1, 0, 2).reshape(768, 1024)
    vmem = pl.BlockSpec(memory_space=pltpu.VMEM)
    hbm = pl.BlockSpec(memory_space=pl.ANY)
    dma = pltpu.SemaphoreType.DMA
    main, rest = pl.pallas_call(
        exchange,
        out_shape=[jax.ShapeDtypeStruct((4, 32, ROWS, WIDE), BF16), jax.ShapeDtypeStruct((32, 32, 128), BF16)],
        in_specs=[vmem] * 3,
        out_specs=[hbm] * 2,
        scratch_shapes=[
            pltpu.VMEM((8, 128, 1024), F32),
            pltpu.VMEM((768, 1024), BF16), pltpu.VMEM((768, 1024), BF16),
            pltpu.VMEM((1152, 1024), BF16), pltpu.VMEM((1152, 1024), BF16),
            pltpu.VMEM((WIDE, 1024), BF16), pltpu.VMEM((WIDE, 1024), BF16),
            pltpu.VMEM((4, 32, ROWS, WIDE), BF16),
            pltpu.VMEM((1024, 128), F32), pltpu.VMEM((32, 32, 128), BF16),
            dma((3, 4)), dma((8,)), dma, dma((4,)), dma((4,)), dma, dma,
        ],
        compiler_params=pltpu.CompilerParams(has_side_effects=True, vmem_limit_bytes=44 << 20),
        cost_estimate=pl.CostEstimate(flops=10_000_000_000, bytes_accessed=8_000_000, transcendentals=0),
    )(coeffs[0], rows, slot)
    pick_main, pick_rest = picks()
    inflow = pl.pallas_call(
        settle,
        grid=(8,),
        out_shape=jax.ShapeDtypeStruct((3, 384, 1024), BF16),
        in_specs=[
            pl.BlockSpec((144, 4 * ROWS), lambda i: (0, 0)),
            pl.BlockSpec((144, 4 * REST), lambda i: (0, 0)),
            pl.BlockSpec((4, 4, ROWS, WIDE), lambda i: (0, i, 0, 0)),
            pl.BlockSpec((4 * REST, 1024), lambda i: (i, 0)),
        ],
        out_specs=pl.BlockSpec((3, 48, 1024), lambda i: (0, i, 0)),
        compiler_params=pltpu.CompilerParams(vmem_limit_bytes=16 << 20),
    )(pick_main, pick_rest, main, rest.reshape(128, 1024))
    return inflow.transpose(1, 0, 2)


def slots(route, capacity):
    owner = route[:, 0]
    place = jnp.arange(owner.shape[0], dtype=jnp.int32)
    before = (owner[:, None] == owner[None, :]) & (place[:, None] < place[None, :])
    return owner * capacity + jnp.sum(before.astype(jnp.int32), axis=0)


def local(coeffs, basis, route):
    points = basis.shape[1]
    count = lax.axis_size(("inlet", "row"))
    capacity = 3 * points // (2 * count)
    panel = lax.all_gather(coeffs, "row", axis=1, tiled=True)[0]
    steps = panel.shape[0]
    slot = slots(route, capacity).reshape(1, points)
    onehot = (jnp.arange(count * capacity, dtype=jnp.int32)[:, None] == slot).astype(jnp.float32)
    packed = jnp.einsum("sp,pcm->csm", onehot, basis[0], precision=lax.Precision.HIGHEST)
    packed = packed.reshape(3, count, capacity, -1).transpose(1, 0, 2, 3).reshape(count * 3 * capacity, -1)
    velocity = jnp.einsum("sm,tm->st", packed, panel, precision=lax.Precision.HIGH)
    velocity = velocity.astype(jnp.bfloat16).reshape(count, 3 * capacity, steps)
    moved = lax.all_to_all(velocity, ("inlet", "row"), split_axis=0, concat_axis=0, tiled=True)
    moved = moved.reshape(count, 3, capacity, steps).transpose(0, 2, 1, 3)
    return moved.reshape(count * capacity, 3, steps)


def solution(mesh):
    sizes = dict(mesh.shape)
    in_specs = (P("inlet", "row", None), P("inlet", "row", None, None), P(("inlet", "row"), None))
    out_specs = P(("inlet", "row"), None, None)

    def body(coeffs, basis, route):
        shapes = (coeffs.shape, basis.shape, route.shape)
        if sizes == {"inlet": 4, "row": 8} and shapes == ((1, 128, 1024), (1, 256, 3, 1024), (256, 1)):
            return fused(coeffs, basis, route)
        return local(coeffs, basis, route)

    return jax.shard_map(body, mesh=mesh, in_specs=in_specs, out_specs=out_specs, check_vma=False)
```

```python
import jax
import jax.numpy as jnp
import numpy as np
from jax import lax
from jax.experimental import pallas as pl
from jax.experimental.pallas import tpu as pltpu
from jax.sharding import PartitionSpec as P

MESH = pl.DeviceIdType.MESH
CAPACITY, ROWS, REST, WIDE = 12, 32, 4, 256
SET = 8
F32, BF16 = jnp.float32, jnp.bfloat16
NT = (((1,), (1,)), ((), ()))


def halves(x):
    high = x.astype(BF16)
    return high, (x - high.astype(F32)).astype(BF16)


def exchange(coeffs, basis, slot, main, rest, panel, base_h, base_l, pack_h, pack_l, pan_h, pan_l, out, rest32, out_rest,
             b_vmem, b_sem, g_send, g_recv, own_sem, a_send, a_recv, x_send, x_recv):
    inlet, row = lax.axis_index("inlet"), lax.axis_index("row")
    me = inlet * 8 + row
    z, core = row // 2, row % 2

    def step(kind, zc, src):
        target = (row + 2, row - 2, z * 2 + 1 - core)[kind]
        return pltpu.make_async_remote_copy(
            src_ref=src, dst_ref=panel.at[zc * 2 + core], send_sem=g_send.at[kind, zc],
            recv_sem=g_recv.at[zc * 2 + core], device_id=(inlet, target), device_id_type=MESH)

    def arrived(chunk):
        pltpu.make_async_copy(panel.at[chunk], panel.at[chunk], g_recv.at[chunk]).wait()

    def sends(zc):
        return ((zc <= z) & (z < 3), (zc >= z) & (z > 0))

    @pl.when(z < 3)
    def _():
        step(0, z, coeffs).start()

    @pl.when(z > 0)
    def _():
        step(1, z, coeffs).start()

    step(2, z, coeffs).start()
    own = pltpu.make_async_copy(coeffs, panel.at[row], own_sem)
    own.start()

    fetch = pltpu.make_async_copy(basis, b_vmem, b_sem)
    fetch.start()
    fetch.wait()

    @pl.loop(0, 3)
    def _(c):
        at = pl.ds(pl.multiple_of(c * 256, 256), 256)
        high, low = halves(b_vmem[at, :])
        base_h[at, :] = high
        base_l[at, :] = low

    owner_of = slot[...]
    named = lax.broadcasted_iota(jnp.int32, (32, 256), 0) == owner_of
    named = jnp.where(named, 1.0, 0.0)
    before = lax.broadcasted_iota(jnp.int32, (256, 256), 0) < lax.broadcasted_iota(jnp.int32, (256, 256), 1)
    before = jnp.where(before, 1.0, 0.0).astype(BF16)
    rank = jnp.sum(named * jnp.dot(named.astype(BF16), before, preferred_element_type=F32), axis=0, keepdims=True)
    points = jnp.broadcast_to(owner_of * CAPACITY + rank.astype(jnp.int32), (128, 256))

    @pl.loop(0, 9)
    def _(tile):
        line = lax.broadcasted_iota(jnp.int32, (128, 256), 0) + tile * 128
        q = line & 31
        c = (q >= 12).astype(jnp.int32) + (q >= 24).astype(jnp.int32)
        key = (line >> 5) * CAPACITY + q - 12 * c
        tail = line - 32 * ROWS
        in_tail = tail >= 0
        key = jnp.where(in_tail, (tail & 31) * CAPACITY + 8 + (tail >> 5), key)
        c = jnp.where(in_tail, 2, c)
        hit = key == points
        pick = jnp.concatenate(
            [jnp.where(hit & (c == k), 1.0, 0.0).astype(BF16) for k in range(3)], axis=1)
        at = pl.ds(pl.multiple_of(tile * 128, 128), 128)
        pack_h[at, :] = jnp.dot(pick, base_h[...], preferred_element_type=F32).astype(BF16)
        pack_l[at, :] = jnp.dot(pick, base_l[...], preferred_element_type=F32).astype(BF16)

    def product(at):
        total = lax.dot_general(pack_h[at, :], pan_h[...], NT, preferred_element_type=F32)
        total += lax.dot_general(pack_l[at, :], pan_h[...], NT, preferred_element_type=F32)
        return total + lax.dot_general(pack_h[at, :], pan_l[...], NT, preferred_element_type=F32)

    def piece(zc, owner):
        return pltpu.make_async_remote_copy(
            src_ref=out.at[zc, owner], dst_ref=main.at[zc, me], send_sem=a_send.at[zc], recv_sem=a_recv.at[zc],
            device_id=(owner // 8, owner % 8), device_id_type=MESH)

    def last(owner):
        return pltpu.make_async_remote_copy(
            src_ref=out_rest.at[owner], dst_ref=rest.at[me], send_sem=x_send, recv_sem=x_recv,
            device_id=(owner // 8, owner % 8), device_id_type=MESH)

    for k in range(4):
        near = [(0, 1, 2, 3), (1, 0, 2, 3), (2, 3, 1, 0), (3, 2, 1, 0)]
        zc = jnp.where(z == 0, near[0][k], jnp.where(z == 1, near[1][k], jnp.where(z == 2, near[2][k], near[3][k])))
        if k == 0:
            own.wait()
        else:
            arrived(zc * 2 + core)
            right, left = sends(zc)

            @pl.when(right)
            def _():
                step(0, zc, panel.at[zc * 2 + core]).start()

            @pl.when(left)
            def _():
                step(1, zc, panel.at[zc * 2 + core]).start()

            step(2, zc, panel.at[zc * 2 + core]).start()
        arrived(zc * 2 + 1 - core)
        for part in range(2):
            high, low = halves(panel[zc * 2 + part])
            pan_h[part * 128:part * 128 + 128, :] = high
            pan_l[part * 128:part * 128 + 128, :] = low

        @pl.loop(0, 4)
        def _(turn):
            group = (turn + inlet) % 4
            at = pl.ds(pl.multiple_of(group * 256, 256), 256)
            out[zc, pl.ds(group * 8, 8)] = product(at).astype(BF16).reshape(8, ROWS, WIDE)

            @pl.loop(0, 8)
            def _(j):
                owner = group * 8 + (j + row) % 8

                @pl.when(owner != me)
                def _():
                    piece(zc, owner).start()

                @pl.when(owner == me)
                def _():
                    pltpu.make_async_copy(out.at[zc, me], main.at[zc, me], a_recv.at[zc]).start()

        tail = product(pl.ds(32 * ROWS, 32 * REST))
        for e in range(REST):
            for part in range(2):
                rest32[pl.ds(e * 8 + zc * 2 + part, 32, stride=32), :] = (
                    tail[e * 32:e * 32 + 32, part * 128:part * 128 + 128])

    out_rest[...] = rest32[...].astype(BF16).reshape(32, 32, 128)

    @pl.loop(0, 32)
    def _(j):
        owner = (j + me) % 32

        @pl.when(owner != me)
        def _():
            last(owner).start()

        @pl.when(owner == me)
        def _():
            pltpu.make_async_copy(out_rest.at[me], rest.at[me], x_recv).start()

    for zc in range(4):
        right, left = sends(zc)

        @pl.when(right)
        def _():
            step(0, zc, coeffs).wait_send()

        @pl.when(left)
        def _():
            step(1, zc, coeffs).wait_send()

        step(2, zc, coeffs).wait_send()
        some = out.at[zc, pl.ds(0, 31)]
        pltpu.make_async_copy(some, some, a_send.at[zc]).wait()
        pltpu.make_async_copy(main.at[zc], main.at[zc], a_recv.at[zc]).wait()
    some = out_rest.at[pl.ds(0, 31)]
    pltpu.make_async_copy(some, some, x_send).wait()
    pltpu.make_async_copy(rest, rest, x_recv).wait()


def settle(pick_main, pick_rest, main, rest, inflow):
    for zc in range(4):
        at = slice(zc * WIDE, zc * WIDE + WIDE)
        block = jnp.dot(pick_main[...], main[zc].reshape(SET * ROWS, WIDE), preferred_element_type=F32)
        block += jnp.dot(pick_rest[...], rest[:, at], preferred_element_type=F32)
        inflow[:, :, at] = block.astype(BF16).reshape(3, SET * CAPACITY, WIDE)


def picks():
    full = np.zeros((SET * 36, SET * 36), np.float32)
    for c in range(3):
        for s in range(SET):
            for r in range(CAPACITY):
                q = c * CAPACITY + r
                full[(c * SET + s) * CAPACITY + r, s * ROWS + q if q < ROWS else SET * ROWS + s * REST + q - ROWS] = 1
    return jnp.asarray(full[:, :SET * ROWS], BF16), jnp.asarray(full[:, SET * ROWS:], BF16)


def fused(coeffs, basis, route):
    slot = route.reshape(1, 256)
    rows = basis[0].transpose(1, 0, 2).reshape(768, 1024)
    vmem = pl.BlockSpec(memory_space=pltpu.VMEM)
    hbm = pl.BlockSpec(memory_space=pl.ANY)
    dma = pltpu.SemaphoreType.DMA
    main, rest = pl.pallas_call(
        exchange,
        out_shape=[jax.ShapeDtypeStruct((4, 32, ROWS, WIDE), BF16), jax.ShapeDtypeStruct((32, 32, 128), BF16)],
        in_specs=[hbm, hbm, vmem],
        out_specs=[hbm] * 2,
        scratch_shapes=[
            pltpu.VMEM((8, 128, 1024), F32),
            pltpu.VMEM((768, 1024), BF16), pltpu.VMEM((768, 1024), BF16),
            pltpu.VMEM((1152, 1024), BF16), pltpu.VMEM((1152, 1024), BF16),
            pltpu.VMEM((WIDE, 1024), BF16), pltpu.VMEM((WIDE, 1024), BF16),
            pltpu.VMEM((4, 32, ROWS, WIDE), BF16),
            pltpu.VMEM((1024, 128), F32), pltpu.VMEM((32, 32, 128), BF16),
            pltpu.VMEM((768, 1024), F32), dma,
            dma((3, 4)), dma((8,)), dma, dma((4,)), dma((4,)), dma, dma,
        ],
        compiler_params=pltpu.CompilerParams(has_side_effects=True, vmem_limit_bytes=60 << 20),
        cost_estimate=pl.CostEstimate(flops=10_000_000_000, bytes_accessed=8_000_000, transcendentals=0),
    )(coeffs[0], rows, slot)
    pick_main, pick_rest = picks()
    inflow = pl.pallas_call(
        settle,
        grid=(32 // SET,),
        out_shape=jax.ShapeDtypeStruct((3, 384, 1024), BF16),
        in_specs=[
            pl.BlockSpec((SET * 36, SET * ROWS), lambda i: (0, 0)),
            pl.BlockSpec((SET * 36, SET * REST), lambda i: (0, 0)),
            pl.BlockSpec((4, SET, ROWS, WIDE), lambda i: (0, i, 0, 0)),
            pl.BlockSpec((SET * REST, 1024), lambda i: (i, 0)),
        ],
        out_specs=pl.BlockSpec((3, SET * CAPACITY, 1024), lambda i: (0, i, 0)),
        compiler_params=pltpu.CompilerParams(vmem_limit_bytes=16 << 20),
    )(pick_main, pick_rest, main, rest.reshape(128, 1024))
    return inflow.transpose(1, 0, 2)


def slots(route, capacity):
    owner = route[:, 0]
    place = jnp.arange(owner.shape[0], dtype=jnp.int32)
    before = (owner[:, None] == owner[None, :]) & (place[:, None] < place[None, :])
    return owner * capacity + jnp.sum(before.astype(jnp.int32), axis=0)


def local(coeffs, basis, route):
    points = basis.shape[1]
    count = lax.axis_size(("inlet", "row"))
    capacity = 3 * points // (2 * count)
    panel = lax.all_gather(coeffs, "row", axis=1, tiled=True)[0]
    steps = panel.shape[0]
    slot = slots(route, capacity).reshape(1, points)
    onehot = (jnp.arange(count * capacity, dtype=jnp.int32)[:, None] == slot).astype(jnp.float32)
    packed = jnp.einsum("sp,pcm->csm", onehot, basis[0], precision=lax.Precision.HIGHEST)
    packed = packed.reshape(3, count, capacity, -1).transpose(1, 0, 2, 3).reshape(count * 3 * capacity, -1)
    velocity = jnp.einsum("sm,tm->st", packed, panel, precision=lax.Precision.HIGH)
    velocity = velocity.astype(jnp.bfloat16).reshape(count, 3 * capacity, steps)
    moved = lax.all_to_all(velocity, ("inlet", "row"), split_axis=0, concat_axis=0, tiled=True)
    moved = moved.reshape(count, 3, capacity, steps).transpose(0, 2, 1, 3)
    return moved.reshape(count * capacity, 3, steps)


def solution(mesh):
    sizes = dict(mesh.shape)
    in_specs = (P("inlet", "row", None), P("inlet", "row", None, None), P(("inlet", "row"), None))
    out_specs = P(("inlet", "row"), None, None)

    def body(coeffs, basis, route):
        shapes = (coeffs.shape, basis.shape, route.shape)
        if sizes == {"inlet": 4, "row": 8} and shapes == ((1, 128, 1024), (1, 256, 3, 1024), (256, 1)):
            return fused(coeffs, basis, route)
        return local(coeffs, basis, route)

    return jax.shard_map(body, mesh=mesh, in_specs=in_specs, out_specs=out_specs, check_vma=False)
```

```python
import jax
import jax.numpy as jnp
import numpy as np
from jax import lax
from jax.experimental import pallas as pl
from jax.experimental.pallas import tpu as pltpu
from jax.sharding import PartitionSpec as P

MESH = pl.DeviceIdType.MESH
CAPACITY, ROWS, REST, WIDE = 12, 32, 4, 256
SET = 8
F32, BF16 = jnp.float32, jnp.bfloat16
NT = (((1,), (1,)), ((), ()))


def halves(x):
    high = x.astype(BF16)
    return high, (x - high.astype(F32)).astype(BF16)


def exchange(coeffs, basis, slot, main, rest, panel, base_h, base_l, pack_h, pack_l, pan_h, pan_l, out, rest32, out_rest,
             b_vmem, b_sem, g_send, g_recv, own_sem, a_send, a_recv, x_send, x_recv):
    inlet, row = lax.axis_index("inlet"), lax.axis_index("row")
    me = inlet * 8 + row
    z, core = row // 2, row % 2

    def step(kind, zc, src, half):
        target = (row + 2, row - 2, z * 2 + 1 - core)[kind]
        return pltpu.make_async_remote_copy(
            src_ref=src.at[pl.ds(half * 64, 64)], dst_ref=panel.at[zc * 2 + core, pl.ds(half * 64, 64)],
            send_sem=g_send.at[kind, zc, half], recv_sem=g_recv.at[zc * 2 + core, half], device_id=(inlet, target), device_id_type=MESH)

    def arrived(chunk, half):
        block = panel.at[chunk, pl.ds(half * 64, 64)]
        pltpu.make_async_copy(block, block, g_recv.at[chunk, half]).wait()

    def sends(zc):
        return ((zc <= z) & (z < 3), (zc >= z) & (z > 0))

    for half in range(2):
        @pl.when(z < 3)
        def _():
            step(0, z, coeffs, half).start()

        @pl.when(z > 0)
        def _():
            step(1, z, coeffs, half).start()

        step(2, z, coeffs, half).start()

    own = pltpu.make_async_copy(coeffs, panel.at[row], own_sem)
    own.start()

    fetch = pltpu.make_async_copy(basis, b_vmem, b_sem)
    fetch.start()
    fetch.wait()

    @pl.loop(0, 3)
    def _(c):
        at = pl.ds(pl.multiple_of(c * 256, 256), 256)
        high, low = halves(b_vmem[at, :])
        base_h[at, :] = high
        base_l[at, :] = low

    owner_of = slot[...]
    named = lax.broadcasted_iota(jnp.int32, (32, 256), 0) == owner_of
    named = jnp.where(named, 1.0, 0.0)
    before = lax.broadcasted_iota(jnp.int32, (256, 256), 0) < lax.broadcasted_iota(jnp.int32, (256, 256), 1)
    before = jnp.where(before, 1.0, 0.0).astype(BF16)
    rank = jnp.sum(named * jnp.dot(named.astype(BF16), before, preferred_element_type=F32), axis=0, keepdims=True)
    points = jnp.broadcast_to(owner_of * CAPACITY + rank.astype(jnp.int32), (128, 256))

    @pl.loop(0, 9)
    def _(tile):
        line = lax.broadcasted_iota(jnp.int32, (128, 256), 0) + tile * 128
        q = line & 31
        c = (q >= 12).astype(jnp.int32) + (q >= 24).astype(jnp.int32)
        key = (line >> 5) * CAPACITY + q - 12 * c
        tail = line - 32 * ROWS
        in_tail = tail >= 0
        key = jnp.where(in_tail, (tail & 31) * CAPACITY + 8 + (tail >> 5), key)
        c = jnp.where(in_tail, 2, c)
        hit = key == points
        pick = jnp.concatenate(
            [jnp.where(hit & (c == k), 1.0, 0.0).astype(BF16) for k in range(3)], axis=1)
        at = pl.ds(pl.multiple_of(tile * 128, 128), 128)
        pack_h[at, :] = jnp.dot(pick, base_h[...], preferred_element_type=F32).astype(BF16)
        pack_l[at, :] = jnp.dot(pick, base_l[...], preferred_element_type=F32).astype(BF16)

    def product(at):
        total = lax.dot_general(pack_h[at, :], pan_h[...], NT, preferred_element_type=F32)
        total += lax.dot_general(pack_l[at, :], pan_h[...], NT, preferred_element_type=F32)
        return total + lax.dot_general(pack_h[at, :], pan_l[...], NT, preferred_element_type=F32)

    def piece(zc, owner):
        return pltpu.make_async_remote_copy(
            src_ref=out.at[zc, owner], dst_ref=main.at[zc, me], send_sem=a_send.at[zc], recv_sem=a_recv.at[zc],
            device_id=(owner // 8, owner % 8), device_id_type=MESH)

    def last(owner):
        return pltpu.make_async_remote_copy(
            src_ref=out_rest.at[owner], dst_ref=rest.at[me], send_sem=x_send, recv_sem=x_recv,
            device_id=(owner // 8, owner % 8), device_id_type=MESH)

    for k in range(4):
        near = [(0, 1, 2, 3), (1, 0, 2, 3), (2, 3, 1, 0), (3, 2, 1, 0)]
        zc = jnp.where(z == 0, near[0][k], jnp.where(z == 1, near[1][k], jnp.where(z == 2, near[2][k], near[3][k])))
        if k == 0:
            own.wait()
        else:
            for half in range(2):
                arrived(zc * 2 + core, half)
                right, left = sends(zc)

                @pl.when(right)
                def _():
                    step(0, zc, panel.at[zc * 2 + core], half).start()

                @pl.when(left)
                def _():
                    step(1, zc, panel.at[zc * 2 + core], half).start()

                step(2, zc, panel.at[zc * 2 + core], half).start()
        for half in range(2):
            arrived(zc * 2 + 1 - core, half)
        for part in range(2):
            high, low = halves(panel[zc * 2 + part])
            pan_h[part * 128:part * 128 + 128, :] = high
            pan_l[part * 128:part * 128 + 128, :] = low

        @pl.loop(0, 4)
        def _(turn):
            group = (turn + inlet) % 4
            at = pl.ds(pl.multiple_of(group * 256, 256), 256)
            out[zc, pl.ds(group * 8, 8)] = product(at).astype(BF16).reshape(8, ROWS, WIDE)

            @pl.loop(0, 8)
            def _(j):
                owner = group * 8 + (j + row) % 8

                @pl.when(owner != me)
                def _():
                    piece(zc, owner).start()

                @pl.when(owner == me)
                def _():
                    pltpu.make_async_copy(out.at[zc, me], main.at[zc, me], a_recv.at[zc]).start()

        tail = product(pl.ds(32 * ROWS, 32 * REST))
        for e in range(REST):
            for part in range(2):
                rest32[pl.ds(e * 8 + zc * 2 + part, 32, stride=32), :] = (
                    tail[e * 32:e * 32 + 32, part * 128:part * 128 + 128])

    out_rest[...] = rest32[...].astype(BF16).reshape(32, 32, 128)

    @pl.loop(0, 32)
    def _(j):
        owner = (j + me) % 32

        @pl.when(owner != me)
        def _():
            last(owner).start()

        @pl.when(owner == me)
        def _():
            pltpu.make_async_copy(out_rest.at[me], rest.at[me], x_recv).start()

    for zc in range(4):
        right, left = sends(zc)

        @pl.when(right)
        def _():
            for half in range(2):
                step(0, zc, coeffs, half).wait_send()

        @pl.when(left)
        def _():
            for half in range(2):
                step(1, zc, coeffs, half).wait_send()

        for half in range(2):
            step(2, zc, coeffs, half).wait_send()
        some = out.at[zc, pl.ds(0, 31)]
        pltpu.make_async_copy(some, some, a_send.at[zc]).wait()
        pltpu.make_async_copy(main.at[zc], main.at[zc], a_recv.at[zc]).wait()
    some = out_rest.at[pl.ds(0, 31)]
    pltpu.make_async_copy(some, some, x_send).wait()
    pltpu.make_async_copy(rest, rest, x_recv).wait()


def settle(pick_main, pick_rest, main, rest, inflow):
    for zc in range(4):
        at = slice(zc * WIDE, zc * WIDE + WIDE)
        block = jnp.dot(pick_main[...], main[zc].reshape(SET * ROWS, WIDE), preferred_element_type=F32)
        block += jnp.dot(pick_rest[...], rest[:, at], preferred_element_type=F32)
        inflow[:, :, at] = block.astype(BF16).reshape(3, SET * CAPACITY, WIDE)


def picks():
    full = np.zeros((SET * 36, SET * 36), np.float32)
    for c in range(3):
        for s in range(SET):
            for r in range(CAPACITY):
                q = c * CAPACITY + r
                full[(c * SET + s) * CAPACITY + r, s * ROWS + q if q < ROWS else SET * ROWS + s * REST + q - ROWS] = 1
    return jnp.asarray(full[:, :SET * ROWS], BF16), jnp.asarray(full[:, SET * ROWS:], BF16)


def fused(coeffs, basis, route):
    slot = route.reshape(1, 256)
    rows = basis[0].transpose(1, 0, 2).reshape(768, 1024)
    vmem = pl.BlockSpec(memory_space=pltpu.VMEM)
    hbm = pl.BlockSpec(memory_space=pl.ANY)
    dma = pltpu.SemaphoreType.DMA
    main, rest = pl.pallas_call(
        exchange,
        out_shape=[jax.ShapeDtypeStruct((4, 32, ROWS, WIDE), BF16), jax.ShapeDtypeStruct((32, 32, 128), BF16)],
        in_specs=[hbm, hbm, vmem],
        out_specs=[hbm] * 2,
        scratch_shapes=[
            pltpu.VMEM((8, 128, 1024), F32),
            pltpu.VMEM((768, 1024), BF16), pltpu.VMEM((768, 1024), BF16),
            pltpu.VMEM((1152, 1024), BF16), pltpu.VMEM((1152, 1024), BF16),
            pltpu.VMEM((WIDE, 1024), BF16), pltpu.VMEM((WIDE, 1024), BF16),
            pltpu.VMEM((4, 32, ROWS, WIDE), BF16),
            pltpu.VMEM((1024, 128), F32), pltpu.VMEM((32, 32, 128), BF16),
            pltpu.VMEM((768, 1024), F32), dma,
            dma((3, 4, 2)), dma((8, 2)), dma, dma((4,)), dma((4,)), dma, dma,
        ],
        compiler_params=pltpu.CompilerParams(has_side_effects=True, vmem_limit_bytes=60 << 20),
        cost_estimate=pl.CostEstimate(flops=10_000_000_000, bytes_accessed=8_000_000, transcendentals=0),
    )(coeffs[0], rows, slot)
    pick_main, pick_rest = picks()
    inflow = pl.pallas_call(
        settle,
        grid=(32 // SET,),
        out_shape=jax.ShapeDtypeStruct((3, 384, 1024), BF16),
        in_specs=[
            pl.BlockSpec((SET * 36, SET * ROWS), lambda i: (0, 0)),
            pl.BlockSpec((SET * 36, SET * REST), lambda i: (0, 0)),
            pl.BlockSpec((4, SET, ROWS, WIDE), lambda i: (0, i, 0, 0)),
            pl.BlockSpec((SET * REST, 1024), lambda i: (i, 0)),
        ],
        out_specs=pl.BlockSpec((3, SET * CAPACITY, 1024), lambda i: (0, i, 0)),
        compiler_params=pltpu.CompilerParams(vmem_limit_bytes=16 << 20),
    )(pick_main, pick_rest, main, rest.reshape(128, 1024))
    return inflow.transpose(1, 0, 2)


def slots(route, capacity):
    owner = route[:, 0]
    place = jnp.arange(owner.shape[0], dtype=jnp.int32)
    before = (owner[:, None] == owner[None, :]) & (place[:, None] < place[None, :])
    return owner * capacity + jnp.sum(before.astype(jnp.int32), axis=0)


def local(coeffs, basis, route):
    points = basis.shape[1]
    count = lax.axis_size(("inlet", "row"))
    capacity = 3 * points // (2 * count)
    panel = lax.all_gather(coeffs, "row", axis=1, tiled=True)[0]
    steps = panel.shape[0]
    slot = slots(route, capacity).reshape(1, points)
    onehot = (jnp.arange(count * capacity, dtype=jnp.int32)[:, None] == slot).astype(jnp.float32)
    packed = jnp.einsum("sp,pcm->csm", onehot, basis[0], precision=lax.Precision.HIGHEST)
    packed = packed.reshape(3, count, capacity, -1).transpose(1, 0, 2, 3).reshape(count * 3 * capacity, -1)
    velocity = jnp.einsum("sm,tm->st", packed, panel, precision=lax.Precision.HIGH)
    velocity = velocity.astype(jnp.bfloat16).reshape(count, 3 * capacity, steps)
    moved = lax.all_to_all(velocity, ("inlet", "row"), split_axis=0, concat_axis=0, tiled=True)
    moved = moved.reshape(count, 3, capacity, steps).transpose(0, 2, 1, 3)
    return moved.reshape(count * capacity, 3, steps)


def solution(mesh):
    sizes = dict(mesh.shape)
    in_specs = (P("inlet", "row", None), P("inlet", "row", None, None), P(("inlet", "row"), None))
    out_specs = P(("inlet", "row"), None, None)

    def body(coeffs, basis, route):
        shapes = (coeffs.shape, basis.shape, route.shape)
        if sizes == {"inlet": 4, "row": 8} and shapes == ((1, 128, 1024), (1, 256, 3, 1024), (256, 1)):
            return fused(coeffs, basis, route)
        return local(coeffs, basis, route)

    return jax.shard_map(body, mesh=mesh, in_specs=in_specs, out_specs=out_specs, check_vma=False)
```
